256 devices in a mesh: leaf: 16 (over x_lo, z), row: 4 (over x_hi, core), col: 4 (over y).
Axes of the slice: x: 4 (x_hi: 2, x_lo: 2; x = x_hi * 2 + x_lo), y: 4, z: 8, core: 2. Of those that a mesh axis runs over, the one named last changes fastest.
Arguments:
- leaf_front: float32 [16, 7, 4, 128, 7, 4, 128], P('leaf', None, 'row', None, None, 'col'), as said below
- leaf_pattern: int32 [16, 28, 28], P('leaf'), may hold values from 0 to 1, as said below
- parent_panel: float32 [2, 16, 7, 4, 128, 4, 128], P(None, 'leaf', None, 'row', None, 'col'), may hold values from -0.125 to 0.125
- parent_diag: float32 [2, 16, 7, 4, 128], P(None, 'leaf', None, 'row'), may hold values from 1.5 to 2.5
- parent_pattern: int32 [2, 16, 28, 28], replicated, may hold values from 0 to 1, as said below
- ext_map: int32 [2, 16, 24], replicated, may hold values from 0 to 27, as said below
Outputs:
- panels: float32 [3, 16, 7, 4, 128, 4, 128], P(None, 'leaf', None, 'row', None, 'col')
- top_update: float32 [16, 6, 4, 128, 6, 4, 128], P('leaf', None, 'row', None, None, 'col')
The draws below stay inside these ranges and needn't reach their ends.
Inputs may be any that keep to these rules, and one draw needn't show every extreme that they name: Each leaf_front[g], read as a matrix, is symmetric; every front built in the reference program is positive definite. leaf_pattern: symmetric, with every diagonal block 1. parent_pattern: symmetric, with every diagonal block 1. parent_pattern[d, n] belongs to node n at depth d+1; rows n of 16 / 2^(d+1) or more are not read. ext_map[d, n] belongs to node n at depth d; rows n of 16 / 2^d or more are not read. Along its 24 entries it rises strictly; ext_map[d, n, j] - j is the same for the 4 entries j of each aligned run of 4, never falls and lies in 0 to 4. Among the entries j of one class of j mod 4, at most two lie in one class of ext_map mod 4, and in every row some two do.
All inputs are finite; a program needn't handle non-finite values.
Results may differ from the reference program's by a relative error of at most 0.0003.
Values sent between devices are 32-bit elements; how exact they have to be, the bound alone decides.
No kernel may reach another device: no remote copies, remote signals or barrier semaphores. Data moves between devices by JAX's collectives and lax.ppermute only.
A program may use at most 128 MiB of HBM per device.

```python
import math
import jax
import jax.numpy as jnp
import numpy as np
from jax import lax

BLOCK = 128
FRONT = 3584
PIVOTS = 512
FRONT_BLOCKS = 28
CONTRIB = 3072
CONTRIB_BLOCKS = 24
BLOCK_ROWS = 7
CONTRIB_ROWS = 6
LEVELS = 2
N_LEAF = 16
N_ROW = 4
N_COL = 4


size_table = np.array([[count_a, count_b, count_c, count_d, count_e] for count_a in range(3) for count_b in range(3) for count_c in range(3) for count_d in range(3) for count_e in range(3) if count_a + count_b + count_c + count_d + count_e == 6 and count_a + count_e <= 2], dtype=np.int32)


def draw_leaf_front(key, part):

    def draw_single(sub_key):
        random_part = jax.random.normal(sub_key, (FRONT, FRONT), jnp.float32)
        diagonal = jax.random.uniform(jax.random.fold_in(sub_key, 1), (FRONT,), jnp.float32, 0.9, 1.5)
        spread_scale = 0.35 / math.sqrt(2.0 * FRONT)
        return (random_part + random_part.T) * spread_scale + jnp.diag(diagonal)
    leaf_keys = jax.random.split(jax.random.fold_in(key, 7), N_LEAF)
    fronts = lax.map(draw_single, leaf_keys)
    return fronts.reshape(N_LEAF, BLOCK_ROWS, N_ROW, BLOCK, BLOCK_ROWS, N_COL, BLOCK)


def pattern_draw(key, leading):
    tosses = jax.random.randint(key, leading + (FRONT_BLOCKS, FRONT_BLOCKS), 0, 5, dtype=jnp.int32)
    row_ids = jnp.arange(FRONT_BLOCKS)[:, None]
    col_ids = jnp.arange(FRONT_BLOCKS)[None, :]
    lower_part = jnp.where(row_ids > col_ids, (tosses < 3).astype(jnp.int32), 0)
    return lower_part + jnp.swapaxes(lower_part, -1, -2) + (row_ids == col_ids).astype(jnp.int32)


def draw_leaf_pattern(key, part):
    return pattern_draw(jax.random.fold_in(key, 11), (N_LEAF,))


def draw_parent_pattern(key, part):
    return pattern_draw(jax.random.fold_in(key, 13), (LEVELS, N_LEAF))


def draw_ext_map(key, part):
    table = jnp.asarray(size_table)
    chosen = jax.random.randint(jax.random.fold_in(key, 17), (LEVELS, N_LEAF), 0, table.shape[0], dtype=jnp.int32)
    counts = table[chosen]
    bounds = jnp.cumsum(counts, axis=-1)
    quad_index = jnp.arange(CONTRIB_BLOCKS // N_ROW, dtype=jnp.int32)
    offsets = jnp.sum((bounds[..., None, :] <= quad_index[:, None]).astype(jnp.int32), axis=-1)
    return jnp.arange(CONTRIB_BLOCKS, dtype=jnp.int32) + jnp.repeat(offsets, N_ROW, axis=-1)


def shard_levels(rng, shape, cuts, low, high):
    factor_of = 1.0
    for axis_at, parts in cuts:
        heights = jax.random.uniform(jax.random.fold_in(jax.random.fold_in(rng, 6), axis_at), (parts,), jnp.float32, low / len(cuts), high / len(cuts))
        factor_of = factor_of * jnp.repeat(jnp.exp(heights), shape[axis_at] // parts).reshape((-1,) + (1,) * (len(shape) - 1 - axis_at))
    return factor_of


def noise(rng, dims, scale, limit, cuts=(), held_as=jnp.bfloat16):
    drawn = scale * jax.random.normal(rng, dims, jnp.float32)
    if cuts:
        drawn = drawn * shard_levels(rng, dims, cuts, -0.22, 0.18)
    return jnp.clip(drawn, -limit, limit).astype(held_as)


def setup_inputs(seed: int = 0) -> dict:
    key_list = jax.random.split(jax.random.key(seed), 7)
    return {
        "leaf_front": draw_leaf_front(jax.random.fold_in(key_list[6], 71), 0),
        "leaf_pattern": draw_leaf_pattern(jax.random.fold_in(key_list[6], 71), 0),
        "parent_panel": noise(key_list[2], (LEVELS, N_LEAF, BLOCK_ROWS, N_ROW, BLOCK, N_COL, BLOCK), (FRONT * 2 // 3) ** -0.5, 0.125, ((1, 16), (3, 4), (5, 4)), jnp.float32),
        "parent_diag": jnp.clip(1.5 + 1.0 * jax.random.uniform(key_list[3], (LEVELS, N_LEAF, BLOCK_ROWS, N_ROW, BLOCK), jnp.float32) ** shard_levels(key_list[3], (LEVELS, N_LEAF, BLOCK_ROWS, N_ROW, BLOCK), ((1, 16), (3, 4)), -0.2, 0.2), 1.5, 2.5),
        "parent_pattern": draw_parent_pattern(jax.random.fold_in(key_list[6], 71), 0),
        "ext_map": draw_ext_map(jax.random.fold_in(key_list[6], 71), 0),
    }


highest = lax.Precision.HIGHEST

def symmetric_lower(matrix):
    return jnp.tril(matrix) + jnp.swapaxes(jnp.tril(matrix, -1), -1, -2)

def partial_factor(front):
    symmetric = symmetric_lower(front)
    pivot_factor = jnp.linalg.cholesky(symmetric[:PIVOTS, :PIVOTS])
    lower_rows = lax.linalg.triangular_solve(pivot_factor, symmetric[PIVOTS:, :PIVOTS], left_side=False, lower=True, transpose_a=True)
    update = symmetric[PIVOTS:, PIVOTS:] - jnp.dot(lower_rows.astype(jnp.float32), lower_rows.T.astype(jnp.float32), precision=highest, preferred_element_type=jnp.float32)
    panel_col = jnp.concatenate([pivot_factor, lower_rows], axis=0)
    return (panel_col, update)

def block_mask(pattern):
    return jnp.repeat(jnp.repeat(pattern.astype(jnp.float32), BLOCK, axis=0), BLOCK, axis=1)

def extend_add(front, update, child_map):
    positions = (child_map[:, None] * BLOCK + jnp.arange(BLOCK, dtype=jnp.int32)[None, :]).reshape(-1).astype(jnp.int32)
    return front.at[positions[:, None], positions[None, :]].add(update)

def reference(leaf_front, leaf_pattern, parent_panel, parent_diag, parent_pattern, ext_map):
    leaves = leaf_front.reshape(N_LEAF, FRONT, FRONT)

    def leaf_step(members):
        front, pattern = members
        return partial_factor(block_mask(pattern) * front)
    panels_now, updates = lax.map(leaf_step, (leaves, leaf_pattern))
    panel_list = [panels_now]
    for depth in range(LEVELS):
        node_count = N_LEAF >> depth + 1
        group_span = 2 ** (depth + 1)
        shares = parent_panel[depth].reshape(node_count, group_span, FRONT, PIVOTS).sum(axis=1)
        diagonals = parent_diag[depth].reshape(node_count, group_span, FRONT).sum(axis=1)
        child_maps = ext_map[depth, :2 * node_count].reshape(node_count, 2, CONTRIB_BLOCKS)
        child_updates = updates.reshape(node_count, 2, CONTRIB, CONTRIB)
        patterns = parent_pattern[depth, :node_count]

        def node_step(members):
            share, diagonal, pattern, maps_here, children = members
            initials = jnp.concatenate([share, jnp.zeros((FRONT, FRONT - PIVOTS), jnp.float32)], axis=1) + jnp.diag(diagonal)
            front = block_mask(pattern) * initials
            front = extend_add(front, children[0], maps_here[0])
            front = extend_add(front, children[1], maps_here[1])
            return partial_factor(front)
        panels_now, updates = lax.map(node_step, (shares, diagonals, patterns, child_maps, child_updates))
        panel_list.append(panels_now)
    stacked = jnp.stack([jnp.repeat(panel_set, 2 ** depth, axis=0) for depth, panel_set in enumerate(panel_list)])
    panels = stacked.reshape(LEVELS + 1, N_LEAF, BLOCK_ROWS, N_ROW, BLOCK, N_COL, BLOCK)
    top_update = jnp.repeat(jnp.tril(updates), 2 ** LEVELS, axis=0).reshape(N_LEAF, CONTRIB_ROWS, N_ROW, BLOCK, CONTRIB_ROWS, N_COL, BLOCK)
    return (panels, top_update)
```

```python
import jax
import jax.numpy as jnp
from jax import lax
from jax.experimental import pallas as pl
from jax.experimental.pallas import tpu as pltpu
from jax.sharding import PartitionSpec as P

side = 4
tile = 8


def dot(left, right, dims=((1,), (0,))):
    return lax.dot_general(
        left,
        right,
        (dims, ((), ())),
        precision=lax.Precision.HIGHEST,
        preferred_element_type=jnp.float32,
    )


def halves(array):
    top = array.astype(jnp.bfloat16)
    return top, (array - top.astype(jnp.float32)).astype(jnp.bfloat16)


def dot_rows(left, right):
    dims = (((1,), (1,)), ((), ()))

    def one(a, b):
        return lax.dot_general(a, b, dims, preferred_element_type=jnp.float32)

    return one(left[0], right[0]) + (one(left[0], right[1]) + one(left[1], right[0]))


def params():
    return pltpu.CompilerParams(vmem_limit_bytes=48 * 2**20)


def vmem():
    return pl.BlockSpec(memory_space=pltpu.VMEM)


def smem():
    return pl.BlockSpec(memory_space=pltpu.SMEM)


def blocks(count, size):
    return jax.ShapeDtypeStruct((count, size, size), jnp.float32)


def low(t, u):
    return t * (t + 1) // 2 + u


def pick(conditions, values, default):
    out = default
    for condition, value in zip(conditions, values):
        out = jnp.where(condition, value, out)
    return out


def shift_of(meta, base, count):
    shift = [meta[base + t] for t in range(count)]
    kind = [s & (side - 1) for s in shift]
    place = []
    for t in range(count):
        place.append(sum([(kind[t] == kind[x]).astype(jnp.int32) for x in range(t)], jnp.int32(0)))
    return shift, kind, place


def run_in_slot(kind, place, want_kind, want_place):
    count = len(kind)
    return pick(
        [(kind[t] == want_kind) & (place[t] == want_place) for t in range(count)],
        range(count),
        jnp.int32(-1),
    )


def parent_rows(shift, mine, count):
    home = []
    for t in range(count):
        origin = (mine - shift[t]) & (side - 1)
        home.append((4 * t + origin + shift[t]) >> 2)
    return [
        pick([home[t] == row for t in range(count)], range(count), jnp.int32(-1))
        for row in range(count + 1)
    ]


def factor_block(block):
    n = block.shape[0]
    groups = [block[tile * i : tile * (i + 1), :] for i in range(n // tile)]
    lane = lax.broadcasted_iota(jnp.int32, (tile, n), 1)
    row_id = lax.broadcasted_iota(jnp.int32, (tile, n), 0)
    lane_one = lax.broadcasted_iota(jnp.int32, (1, n), 1)
    pivots = []
    for g in range(n // tile):
        base = tile * g
        cols = [
            [
                jnp.broadcast_to(groups[i][:, base + k : base + k + 1], (tile, n))
                for i in range(g, n // tile)
            ]
            for k in range(tile)
        ]
        in_panel = jnp.logical_and(lane >= base, lane < base + tile)
        for i in range(g + 1, n // tile):
            groups[i] = jnp.where(in_panel, 0.0, groups[i])
        own = groups[g]
        pivot = jnp.ones((tile, n), jnp.float32)
        for k in range(tile):
            value = cols[k][0][k : k + 1, :]
            pivot = jnp.where(row_id == k, value, pivot)
            scale = 1.0 / value
            row = jnp.where(lane_one == base + k, 1.0, own[k : k + 1, :])
            row_below = jnp.where(
                jnp.logical_and(lane_one > base + k, lane_one < base + tile), 0.0, row
            )
            ratio = jnp.where(row_id > k, cols[k][0] * scale, 0.0)
            for later in range(k + 1, tile):
                cols[later][0] = cols[later][0] - ratio * cols[later][0][k : k + 1, :]
            own = (
                jnp.where(jnp.logical_and(lane == base + k, row_id > k), 0.0, own) - ratio * row
            )
            for x in range(1, n // tile - g):
                ratio = cols[k][x] * scale
                for later in range(k + 1, tile):
                    cols[later][x] = cols[later][x] - ratio * cols[later][0][k : k + 1, :]
                groups[g + x] = groups[g + x] - ratio * row_below
        groups[g] = own
        pivots.append(pivot)
    upper, inverse = [], []
    for g in range(n // tile):
        scale = lax.rsqrt(pivots[g])
        rows = row_id + tile * g
        upper.append(
            jnp.where(lane > rows, groups[g], jnp.where(lane == rows, pivots[g], 0.0)) * scale
        )
        inverse.append(
            jnp.where(lane < rows, groups[g], jnp.where(lane == rows, 1.0, 0.0)) * scale
        )
    return jnp.concatenate(upper, 0), jnp.concatenate(inverse, 0)


def factor_in_place(work, lower, inverse_t, size):
    count = work.shape[0] // size
    order = work.shape[0]
    lower[...] = jnp.zeros_like(lower)
    inverse_t[...] = jnp.zeros_like(inverse_t)

    def step(b, carry):
        at = pl.ds(pl.multiple_of(b * size, size), size)
        upper, inverse = factor_block(work[at, at])
        lower[at, at] = upper.T
        work[at, at] = jnp.eye(size, dtype=jnp.float32)
        wide = dot(inverse, work[at, :])
        work[at, :] = wide

        def rest(c, inner):
            there = pl.ds(pl.multiple_of(c * size, size), size)
            part = work[at, there].T
            lower[there, at] = part
            work[there, at] = jnp.zeros((size, size), jnp.float32)
            work[there, :] -= dot(part, work[at, :])
            return inner

        lax.fori_loop(b + 1, count, rest, 0)

        def save(c, inner):
            there = pl.ds(pl.multiple_of(c * size, size), size)
            inverse_t[there, at] = work[at, there].T
            return inner

        lax.fori_loop(0, b + 1, save, 0)
        return carry

    lax.fori_loop(0, count, step, 0)


def corner_body(meta, q0, q1, q2, q3, block_out, inverse_out, full, work, lower):
    size = block_out.shape[0]
    my_row, my_col = meta[0], meta[1]
    for back_row, ref in enumerate((q0, q1, q2, q3)):
        at_row = pl.ds(pl.multiple_of(((my_row - back_row) & 3) * size, size), size)
        for back_col in range(side):
            at_col = pl.ds(pl.multiple_of(((my_col - back_col) & 3) * size, size), size)
            full[at_row, at_col] = ref[back_col]
    rows = lax.broadcasted_iota(jnp.int32, (size, size), 0)
    cols = lax.broadcasted_iota(jnp.int32, (size, size), 1)
    work[...] = jnp.zeros_like(work)
    for b in range(side):
        at = slice(b * size, (b + 1) * size)
        for c in range(b, side):
            there = slice(c * size, (c + 1) * size)
            block = full[there, at]
            work[at, there] = jnp.where(rows >= cols, block, block.T) if b == c else block.T
    factor_in_place(work, lower, inverse_out, size)
    at_row = pl.ds(pl.multiple_of(my_row * size, size), size)
    at_col = pl.ds(pl.multiple_of(my_col * size, size), size)
    block_out[...] = lower[at_row, at_col]


def factor_corner(meta, quads):
    size = quads[0].shape[-1]
    order = side * size
    return pl.pallas_call(
        corner_body,
        in_specs=[smem()] + [vmem()] * 4,
        out_specs=[vmem()] * 2,
        out_shape=(
            jax.ShapeDtypeStruct((size, size), jnp.float32),
            jax.ShapeDtypeStruct((order, order), jnp.float32),
        ),
        scratch_shapes=[pltpu.VMEM((order, order), jnp.float32)] * 3,
        compiler_params=params(),
        cost_estimate=pl.CostEstimate(flops=3 * 10**9, bytes_accessed=8 * 10**7, transcendentals=0),
        name="factor_corner",
    )(meta, *quads)


def update_body(where, meta, r0, r1, r2, r3, c0, c1, c2, c3, inverse_t, front, panel, update, rows, cols):
    count, size = panel.shape[0], panel.shape[1]
    my_row, my_col = meta[0], meta[1]
    for back in range(side):
        at_col = pl.ds(pl.multiple_of(((my_col - back) & 3) * size, size), size)
        at_row = pl.ds(pl.multiple_of(((my_row - back) & 3) * size, size), size)
        for t in range(count):
            here = slice(t * size, (t + 1) * size)
            rows[here, at_col] = (r0, r1, r2, r3)[back][t]
            cols[here, at_row] = (c0, c1, c2, c3)[back][t]
    rows[...] = dot(rows[...], inverse_t[...])
    cols[...] = dot(cols[...], inverse_t[...])
    mine = pl.ds(pl.multiple_of(my_col * size, size), size)
    for t in range(count):
        panel[t] = rows[t * size : (t + 1) * size, mine]
    across = halves(cols[...])
    for t in range(count):
        here = halves(rows[t * size : (t + 1) * size, :])
        end = (t + 1) * size
        product = dot_rows(here, (across[0][:end], across[1][:end]))
        for u in range(t + 1):
            update[low(t, u)] = (
                front[where[low(t, u)]] - product[:, u * size : (u + 1) * size]
            )


def update_call(where, meta, row_parts, col_parts, inverse_t, front):
    count, size = row_parts[0].shape[0], row_parts[0].shape[1]
    order = side * size
    return pl.pallas_call(
        update_body,
        in_specs=[smem()] * 2 + [vmem()] * 10,
        out_specs=[vmem()] * 2,
        out_shape=(blocks(count, size), blocks(low(count, 0), size)),
        scratch_shapes=[pltpu.VMEM((count * size, order), jnp.float32)] * 2,
        compiler_params=params(),
        cost_estimate=pl.CostEstimate(
            flops=8 * 10**9, bytes_accessed=15 * 10**6, transcendentals=0
        ),
        name="panel_update",
    )(where, meta, *row_parts, *col_parts, inverse_t, front)


def send_slots(meta, get, slots, send):
    count = 6
    my_row, my_col = meta[0], meta[1]
    _, kind, place = shift_of(meta, 2, count)
    table = [[run_in_slot(kind, place, k, i) for i in range(2)] for k in range(side)]
    for k in range(side):
        for i in range(2):
            t = table[k][i]

            @pl.when(t >= 0)
            def _():
                slots[2 * k + i] = get(t + 1, 0)

    for a in range(side):
        for b in range(side):
            device = ((my_row + a) & 3) * side + ((my_col + b) & 3)
            for i in range(2):
                for j in range(2):
                    t, u = table[a][i], table[b][j]

                    @pl.when((u >= 0) & (t >= u))
                    def _():
                        send[device, 2 * i + j] = get(t + 1, u + 1)


def leaf_body(meta, pattern, front, first, slots, send):
    size = first.shape[1]
    my_row, my_col = meta[0], meta[1]

    def get(t, u):
        keep = pattern[4 * t + my_row, 4 * u + my_col].astype(jnp.float32)
        return keep * front[pl.ds(pl.multiple_of(t * size, size), size), pl.ds(pl.multiple_of(u * size, size), size)]

    first[0] = get(0, 0)
    send_slots(meta, get, slots, send)


def leaf_call(meta, pattern, front, size):
    return pl.pallas_call(
        leaf_body,
        in_specs=[smem()] * 2 + [vmem()],
        out_specs=[vmem()] * 3,
        out_shape=(
            blocks(1, size),
            blocks(2 * side, size),
            jax.ShapeDtypeStruct((side * side, 4, size, size), jnp.float32),
        ),
        compiler_params=params(),
        cost_estimate=pl.CostEstimate(flops=10**6, bytes_accessed=8 * 10**6, transcendentals=0),
        name="leaf_pack",
    )(meta, pattern, front)


def merged_blocks(maps, pattern, own, other, share_a, share_b, diag_a, diag_b):
    count = 6
    size = own.shape[1]
    my_row, my_col = maps[0], maps[1]
    tables = []
    for base in (2, 2 + count):
        shift, _, _ = shift_of(maps, base, count)
        tables.append((parent_rows(shift, my_row, count), parent_rows(shift, my_col, count)))
    same = lax.broadcasted_iota(jnp.int32, (size, size), 0) == lax.broadcasted_iota(
        jnp.int32, (size, size), 1
    )

    def fill(t, u, target, index):
        keep = pattern[4 * t + my_row, 4 * u + my_col].astype(jnp.float32)
        if u == 0:
            target[index] = keep * (share_a[t] + share_b[t])
        else:
            target[index] = jnp.zeros((size, size), jnp.float32)
        if t == u:

            @pl.when(my_row == my_col)
            def _():
                entries = diag_a[t : t + 1, :] + diag_b[t : t + 1, :]
                target[index] += jnp.where(same, keep * entries, 0.0)

        for (to_row, to_col), source in zip(tables, (own, other)):
            x, y = to_row[t], to_col[u]

            @pl.when((y >= 0) & (x >= y))
            def _():
                target[index] += source[(x * (x + 1) >> 1) + y]

    return fill


def merge_body(maps, meta, pattern, own, other, share_a, share_b, diag_a, diag_b, first, slots, send, front):
    fill = merged_blocks(maps, pattern, own, other, share_a, share_b, diag_a, diag_b)
    for t in range(7):
        for u in range(t + 1):
            fill(t, u, front, low(t, u))
    first[0] = front[0]

    def get(t, u):
        return front[(t * (t + 1) >> 1) + u]

    send_slots(meta, get, slots, send)


def merge_call(maps, meta, pattern, own, other, share_a, share_b, diag_a, diag_b):
    size = own.shape[1]
    return pl.pallas_call(
        merge_body,
        in_specs=[smem()] * 3 + [vmem()] * 6,
        out_specs=[vmem()] * 3,
        out_shape=(
            blocks(1, size),
            blocks(2 * side, size),
            jax.ShapeDtypeStruct((side * side, 4, size, size), jnp.float32),
        ),
        scratch_shapes=[pltpu.VMEM((28, size, size), jnp.float32)],
        compiler_params=params(),
        cost_estimate=pl.CostEstimate(flops=10**6, bytes_accessed=10**7, transcendentals=0),
        name="merge_pack",
    )(maps, meta, pattern, own, other, share_a, share_b, diag_a, diag_b)


def merge_last_body(maps, pattern, own, other, share_a, share_b, diag_a, diag_b, first, column, front):
    fill = merged_blocks(maps, pattern, own, other, share_a, share_b, diag_a, diag_b)
    fill(0, 0, first, 0)
    for t in range(1, 7):
        fill(t, 0, column, t - 1)
        for u in range(1, t + 1):
            fill(t, u, front, low(t - 1, u - 1))


def merge_last_call(maps, pattern, own, other, share_a, share_b, diag_a, diag_b):
    size = own.shape[1]
    return pl.pallas_call(
        merge_last_body,
        in_specs=[smem()] * 2 + [vmem()] * 6,
        out_specs=[vmem()] * 3,
        out_shape=(blocks(1, size), blocks(6, size), blocks(21, size)),
        compiler_params=params(),
        cost_estimate=pl.CostEstimate(flops=10**6, bytes_accessed=10**7, transcendentals=0),
        name="merge_last",
    )(maps, pattern, own, other, share_a, share_b, diag_a, diag_b)


def settle_body(meta, s0, s1, s2, s3, out):
    count = out.shape[0]
    _, kind, place = shift_of(meta, 2, count)
    for t in range(count):
        for k, ref in enumerate((s0, s1, s2, s3)):

            @pl.when(kind[t] == k)
            def _():
                out[t] = ref[place[t]]


def settle_call(meta, parts, count):
    size = parts[0].shape[1]
    return pl.pallas_call(
        settle_body,
        in_specs=[smem()] + [vmem()] * 4,
        out_specs=vmem(),
        out_shape=blocks(count, size),
        compiler_params=params(),
        name="settle",
    )(meta, *parts)


def slots_body(meta, column, slots):
    _, kind, place = shift_of(meta, 2, column.shape[0])
    for t in range(column.shape[0]):
        slots[2 * kind[t] + place[t]] = column[t]


def slots_call(meta, column):
    return pl.pallas_call(
        slots_body,
        in_specs=[smem(), vmem()],
        out_specs=vmem(),
        out_shape=blocks(2 * side, column.shape[1]),
        compiler_params=params(),
        name="slots",
    )(meta, column)


def rotate(array, axis, by):
    return lax.ppermute(array, axis, [(i, (i + by) % side) for i in range(side)])


def transpose_grid(array):
    route = [(i * side + j, j * side + i) for i in range(side) for j in range(side)]
    return lax.ppermute(array, ("row", "col"), route)


def across(array, bit):
    count = lax.axis_size("leaf")
    return lax.ppermute(array, "leaf", [(i, i ^ (1 << bit)) for i in range(count)])


def around(array, axis):
    return [array] + [rotate(array, axis, k) for k in range(1, side)]


def corner_parts(first):
    strip = jnp.concatenate(around(first, "col"), 0)
    return around(strip, "row")


def shift_slots(slots, sign):
    parts = [slots[2 * k : 2 * k + 2] for k in range(side)]
    return [parts[0]] + [rotate(parts[k], "row", sign * k) for k in range(1, side)]


def shards(leaf_front, leaf_pattern, parent_panel, parent_diag, parent_pattern, ext_map):
    block_rows = leaf_front.shape[1]
    size = leaf_front.shape[3]
    count = block_rows - 1
    levels = parent_panel.shape[0]
    my_row = lax.axis_index("row").astype(jnp.int32)
    my_col = lax.axis_index("col").astype(jnp.int32)
    my_leaf = lax.axis_index("leaf")
    here = jnp.stack([my_row, my_col])
    runs = ext_map.reshape(levels, -1, count, side)[..., 0] - side * jnp.arange(count, dtype=jnp.int32)

    def shift_row(depth, node):
        return lax.dynamic_index_in_dim(runs[depth], node, 0, keepdims=False)

    metas, maps, wheres = [], [], []
    for depth in range(levels):
        node = jnp.right_shift(my_leaf, depth)
        own = shift_row(depth, node)
        metas.append(jnp.concatenate([here, own]))
        maps.append(jnp.concatenate([here, own, shift_row(depth, node ^ 1)]))
        kind = own % side
        ids = jnp.arange(count)
        place = jnp.sum(
            ((kind[:, None] == kind[None, :]) & (ids[:, None] > ids[None, :])).astype(jnp.int32), 1
        )
        from_row = (my_row - own) % side
        from_col = (my_col - own) % side
        table = (from_row[:, None] * side + from_col[None, :]) * 4 + 2 * place[:, None] + place[None, :]
        wheres.append(jnp.concatenate([table[t, : t + 1] for t in range(count)]))
    wheres.append(jnp.arange(low(count, 0), dtype=jnp.int32))
    metas.append(jnp.concatenate([here, jnp.zeros((count,), jnp.int32)]))
    patterns = [leaf_pattern[0]] + [
        lax.dynamic_index_in_dim(
            parent_pattern[depth], jnp.right_shift(my_leaf, depth + 1), 0, keepdims=False
        )
        for depth in range(levels)
    ]

    share = parent_panel.reshape(levels, block_rows, size, size)
    diag = parent_diag.reshape(levels, block_rows, size)
    pairs = []
    for depth in range(levels):
        other_share, other_diag = across((share, diag), depth)
        pairs.append((share[0], other_share[0], diag[0], other_diag[0]))
        if depth + 1 < levels:
            share, diag = share[1:] + other_share[1:], diag[1:] + other_diag[1:]

    panel_list = []
    first, slots, send = leaf_call(
        metas[0], patterns[0], leaf_front.reshape(block_rows * size, block_rows * size), size
    )
    column = None
    for level in range(levels + 1):
        quads = corner_parts(first)
        if level < levels:
            front = lax.all_to_all(send, ("row", "col"), split_axis=0, concat_axis=0, tiled=True)
            front = front.reshape(-1, size, size)
            column = settle_call(metas[level], shift_slots(slots, 1), count)
        row_parts = around(column, "col")
        col_parts = around(transpose_grid(column), "row")
        top, inverse_t = factor_corner(metas[level], quads)
        panel, update = update_call(
            wheres[level], metas[level], row_parts, col_parts, inverse_t, front
        )
        if level < levels:
            other = across(update, level)
            args = (maps[level], metas[level + 1], patterns[level + 1], update, other) + pairs[level]
            if level + 1 < levels:
                first, slots, send = merge_call(*args)
            else:
                first, column, front = merge_last_call(args[0], *args[2:])
            panel = settle_call(
                metas[level], shift_slots(slots_call(metas[level], panel), -1), count
            )
        panel_list.append(jnp.concatenate([top[None], panel], 0))
    panels = jnp.stack(panel_list).reshape(levels + 1, 1, block_rows, 1, size, 1, size)
    ids = jnp.arange(size)
    rows = []
    for t in range(count):
        line = []
        for u in range(count):
            if t < u:
                line.append(jnp.zeros((size, size), jnp.float32))
            elif t == u:
                keep = (my_row * size + ids)[:, None] >= (my_col * size + ids)[None, :]
                line.append(jnp.where(keep, update[low(t, u)], 0.0))
            else:
                line.append(update[low(t, u)])
        rows.append(jnp.stack(line, 1))
    top_update = jnp.stack(rows).reshape(1, count, 1, size, count, 1, size)
    return (panels, top_update)


def solution(mesh):
    return jax.shard_map(
        shards,
        mesh=mesh,
        in_specs=(
            P("leaf", None, "row", None, None, "col", None),
            P("leaf", None, None),
            P(None, "leaf", None, "row", None, "col", None),
            P(None, "leaf", None, "row", None),
            P(),
            P(),
        ),
        out_specs=(
            P(None, "leaf", None, "row", None, "col", None),
            P("leaf", None, "row", None, None, "col", None),
        ),
        check_vma=False,
    )
```
